32 devices in a mesh: blk: 4 (over y, x), head: 8 (over z, core).
Axes of the slice: x: 2, y: 2, z: 4, core: 2. Of those that a mesh axis runs over, the one named last changes fastest.
Arguments:
- qkv: bfloat16 [16384, 6144], P(('blk', 'head')), may hold values from -12 to 12
Outputs:
- attended: bfloat16 [16384, 2048], P(('blk', 'head'))
The draws below stay inside these ranges and needn't reach their ends.
All inputs are finite; a program needn't handle non-finite values.
Results may differ from the reference program's by a relative error of at most 0.0059.
Values may be sent and summed in bfloat16 or wider, within the bound.
No kernel may reach another device: no remote copies, remote signals or barrier semaphores. Data moves between devices by JAX's collectives and lax.ppermute only.
A program may use at most 128 MiB of HBM per device.

```python
import jax
import jax.numpy as jnp
from jax import lax

HEADS = 32
HEAD_DIM = 64
BLOCK = 2048
D = 2048
TOKENS = 16384


def draw_qkv(key, part):
    first = jax.random.fold_in(key, 0)
    base = jnp.clip(jax.random.normal(first, (TOKENS, 3 * D), jnp.float32), -6.0, 6.0)
    return base.astype(jnp.bfloat16)


def setup_inputs(seed: int = 0) -> dict:
    arg_keys = jax.random.split(jax.random.key(seed), 2)
    return {
        "qkv": draw_qkv(jax.random.fold_in(arg_keys[1], 71), 0),
    }


def one_head(parts):
    nblk = TOKENS // BLOCK
    steps = nblk.bit_length() - 1
    scale = HEAD_DIM ** -0.5
    results = []
    for block_a in range(nblk):
        query = parts[0, block_a]
        partners = [block_a] + [block_a ^ (1 << i) for i in range(steps)]
        maxima, totals, values = [], [], []
        for block_c in partners:
            scores = jnp.dot(query, parts[1, block_c].T, preferred_element_type=jnp.float32) * scale
            row_max = jnp.max(scores, axis=1, keepdims=True)
            probs = jnp.exp(scores - row_max).astype(jnp.bfloat16)
            totals.append(jnp.sum(probs.astype(jnp.float32), axis=1, keepdims=True))
            values.append(jnp.dot(probs, parts[2, block_c], preferred_element_type=jnp.float32))
            maxima.append(row_max)
        overall = maxima[0]
        for row_max in maxima[1:]:
            overall = jnp.maximum(overall, row_max)
        numer = jnp.zeros_like(values[0])
        denom = jnp.zeros_like(totals[0])
        for row_max, total, value in zip(maxima, totals, values):
            factor = jnp.exp(row_max - overall)
            numer = numer + factor * value
            denom = denom + factor * total
        results.append(numer / denom)
    return jnp.stack(results)


def reference(qkv):
    nblk = TOKENS // BLOCK
    grid = qkv.reshape(nblk, BLOCK, 3, HEADS, HEAD_DIM).transpose(3, 2, 0, 1, 4)
    result = lax.map(one_head, grid)
    return result.transpose(1, 2, 0, 3).reshape(TOKENS, D).astype(jnp.bfloat16)
```

```python
import functools

import jax
import jax.numpy as jnp
from jax import lax
from jax.experimental import pallas as pl
from jax.experimental.pallas import tpu as pltpu
from jax.sharding import PartitionSpec as P

HEAD_DIM = 64
LANES = 128
BLOCK = 2048
HEAD_ROWS = 80
LIMIT = 1e30
F32 = jnp.float32
BF16 = jnp.bfloat16
NT = (((1,), (1,)), ((), ()))
ANY = pl.BlockSpec(memory_space=pl.ANY)


def params(mib=40):
    return pltpu.CompilerParams(vmem_limit_bytes=mib << 20)


def cost(units):
    return pl.CostEstimate(flops=int(units * 1e10), bytes_accessed=1 << 20, transcendentals=0)


def staged(moves, buf_ref, in_sem, out_sem):
    reads = [pltpu.make_async_copy(s, buf_ref.at[n], in_sem) for n, (s, _) in enumerate(moves)]
    writes = [pltpu.make_async_copy(buf_ref.at[n], d, out_sem) for n, (_, d) in enumerate(moves)]
    for copy in reads:
        copy.start()
    for copy in reads:
        copy.wait()
    for copy in writes:
        copy.start()
    for copy in writes:
        copy.wait()


def move(kernel, rank, arrays, out_shape, n, rows, units, aliases=None):
    many = isinstance(out_shape, list)
    n_in, n_out = len(arrays), len(out_shape) if many else 1

    def body(rank_ref, *refs):
        ins, outs, rest = refs[:n_in], refs[n_in : n_in + n_out], refs[n_in + n_out :]
        staged(kernel(rank_ref[0], ins, outs), *rest)

    return pl.pallas_call(
        body,
        in_specs=[pl.BlockSpec(memory_space=pltpu.SMEM)] + [ANY] * n_in,
        out_specs=[ANY] * n_out if many else ANY,
        out_shape=out_shape,
        scratch_shapes=[
            pltpu.VMEM((n, rows, LANES), BF16),
            pltpu.SemaphoreType.DMA,
            pltpu.SemaphoreType.DMA,
        ],
        input_output_aliases=aliases or {},
        compiler_params=params(),
        cost_estimate=cost(units),
    )(rank, *arrays)


def pack(rank, qkv, first, groups, order):
    rows = qkv.shape[0]
    width = qkv.shape[1] // 3

    def kernel(me, ins, outs):
        moves = []
        for out, (kinds, dest) in zip(outs, order):
            for at, k in enumerate(dest):
                owner = k if isinstance(k, int) else jnp.bitwise_xor(me, k[0])
                start = pl.multiple_of(owner * (width // groups) + first * LANES, LANES)
                for n, kind in enumerate(kinds):
                    moves.append((ins[0].at[:, pl.ds(kind * width + start, LANES)], out.at[at, n]))
        return moves

    shapes = [(len(dest), len(kinds), rows, LANES) for kinds, dest in order]
    n = sum(shape[0] * shape[1] for shape in shapes)
    shapes = [jax.ShapeDtypeStruct(shape, BF16) for shape in shapes]
    return move(kernel, rank, [qkv], shapes, n, rows, 0.2)


def merge(rank, pieces):
    rows, n = pieces[0].shape[2], len(pieces)

    def kernel(me, ins, outs):
        q, kv = outs
        moves = [(ins[k].at[0, 1 + i], kv.at[k, i]) for k in range(n) for i in range(2)]
        return moves + [(ins[k].at[0, 0], q.at[jnp.bitwise_xor(me, k)]) for k in range(n)]

    shapes = [(n, rows, LANES), (n, 2, rows, LANES)]
    shapes = [jax.ShapeDtypeStruct(shape, BF16) for shape in shapes]
    return move(kernel, rank, pieces, shapes, 3 * n, rows, 0.2)


def regroup(rank, arrays):
    groups, rows, _ = arrays[0].shape
    n = len(arrays)

    def kernel(me, ins, outs):
        return [
            (ins[p].at[jnp.bitwise_xor(me, k)], out.at[p])
            for k, out in enumerate(outs)
            for p in range(n)
        ]

    shapes = [jax.ShapeDtypeStruct((n, rows, LANES), BF16)] * groups
    return move(kernel, rank, arrays, shapes, n * groups, rows, 0.2)


def place_early(rank, pieces, shape):
    n, rows, _ = pieces[0].shape
    width = shape[1] // len(pieces)

    def kernel(me, ins, outs):
        moves = []
        for k, piece in enumerate(ins):
            for p in range(n):
                start = pl.multiple_of(jnp.bitwise_xor(me, k) * width + p * LANES, LANES)
                moves.append((piece.at[p], outs[0].at[:, pl.ds(start, LANES)]))
        return moves

    out = jax.ShapeDtypeStruct(shape, BF16)
    return move(kernel, rank, pieces, out, n * len(pieces), rows, 0.2)


def place_last(rank, pieces, base, pair):
    groups, rows, _ = pieces.shape
    width = base.shape[1] // groups

    def kernel(me, ins, outs):
        return [
            (ins[0].at[k], outs[0].at[:, pl.ds(k * width + pair * LANES, LANES)])
            for k in range(groups)
        ]

    out = jax.ShapeDtypeStruct(base.shape, BF16)
    return move(kernel, rank, [pieces, base], out, groups, rows, 0.1, {2: 0})


def prepare(kv_refs, keys_ref, values_ref):
    tokens = keys_ref.shape[2]
    rows = kv_refs[0].shape[2]
    pieces = [(ref, g) for ref in kv_refs for g in range(ref.shape[0])]
    for n, (kv_ref, g) in enumerate(pieces):
        slot, at = divmod(n * rows, tokens)
        keys = kv_ref[g, 0]
        lane = lax.broadcasted_iota(jnp.int32, keys.shape, 1)
        one = jnp.ones_like(keys)
        span = pl.ds(at, rows)
        keys_ref[slot, 0, span, :] = jnp.where(lane < HEAD_DIM, keys, one)
        keys_ref[slot, 1, span, :] = jnp.where(lane < HEAD_DIM, one, keys)
        values = kv_ref[g, 1].T
        for h in range(2):
            values_ref[slot, h, :HEAD_DIM, span] = values[h * HEAD_DIM : (h + 1) * HEAD_DIM]
            values_ref[slot, h, HEAD_DIM:, span] = jnp.ones((HEAD_ROWS - HEAD_DIM, rows), BF16)


def weigh(keys, values, query):
    scores = lax.dot_general(keys, query, NT, preferred_element_type=F32)
    probs = jnp.exp(scores).astype(BF16)
    return jnp.dot(values, probs, preferred_element_type=F32)


def first_kernel(q_ref, kv_ref, qe_ref, acc_ref, keys_ref, values_ref):
    h = pl.program_id(1)

    @pl.when((pl.program_id(0) == 0) & (h == 0))
    def _():
        prepare([kv_ref], keys_ref, values_ref)

    query = q_ref[...] * jnp.asarray(HEAD_DIM**-0.5, BF16)
    lane = lax.broadcasted_iota(jnp.int32, query.shape, 1)
    mine = (lane // HEAD_DIM) == h
    query = jnp.where(mine, query, jnp.zeros_like(query))
    probe = 256
    some = lax.dot_general(query, keys_ref[0, h, :probe, :], NT, preferred_element_type=F32)
    shift = -jnp.max(some, axis=1, keepdims=True)
    query = jnp.where(lane == (1 - h) * HEAD_DIM, shift.astype(BF16), query)
    qe_ref[0] = query
    acc_ref[0] = weigh(keys_ref[0, h], values_ref[0, h], query)


def first(q, kv):
    tokens = q.shape[0] * q.shape[1]
    tile = min(512, tokens)
    return pl.pallas_call(
        first_kernel,
        grid=(tokens // tile, 2),
        in_specs=[
            pl.BlockSpec((tile, LANES), lambda i, h: (i, 0)),
            pl.BlockSpec(kv.shape, lambda i, h: (0, 0, 0, 0)),
        ],
        out_specs=[
            pl.BlockSpec((1, tile, LANES), lambda i, h: (h, i, 0)),
            pl.BlockSpec((1, HEAD_ROWS, tile), lambda i, h: (h, 0, i)),
        ],
        out_shape=[
            jax.ShapeDtypeStruct((2, tokens, LANES), BF16),
            jax.ShapeDtypeStruct((2, HEAD_ROWS, tokens), F32),
        ],
        scratch_shapes=[
            pltpu.VMEM((1, 2, tokens, LANES), BF16),
            pltpu.VMEM((1, 2, HEAD_ROWS, tokens), BF16),
        ],
        compiler_params=params(),
        cost_estimate=cost(1),
    )(q.reshape(tokens, LANES), kv)


def blocks_of(kvs, tokens):
    return sum(kv.shape[0] * kv.shape[2] for kv in kvs) // tokens


def more_kernel(qe_ref, acc_ref, *refs, n_refs, n):
    kv_refs, (out_ref, keys_ref, values_ref) = refs[:n_refs], refs[n_refs:]
    h = pl.program_id(1)

    @pl.when((pl.program_id(0) == 0) & (h == 0))
    def _():
        prepare(kv_refs, keys_ref, values_ref)

    query = qe_ref[0]
    out_ref[0] = acc_ref[0]

    def step(slot, carry):
        out_ref[0] += weigh(keys_ref[slot, h], values_ref[slot, h], query)
        return carry

    lax.fori_loop(0, n, step, 0)


def more(qe, acc, kvs):
    tokens = qe.shape[1]
    n = blocks_of(kvs, tokens)
    tile = min(512, tokens)
    state = pl.BlockSpec((1, HEAD_ROWS, tile), lambda i, h: (h, 0, i))
    return pl.pallas_call(
        functools.partial(more_kernel, n_refs=len(kvs), n=n),
        grid=(tokens // tile, 2),
        in_specs=[pl.BlockSpec((1, tile, LANES), lambda i, h: (h, i, 0)), state]
        + [pl.BlockSpec(kv.shape, lambda i, h: (0, 0, 0, 0)) for kv in kvs],
        out_specs=state,
        out_shape=jax.ShapeDtypeStruct(acc.shape, F32),
        scratch_shapes=[
            pltpu.VMEM((n, 2, tokens, LANES), BF16),
            pltpu.VMEM((n, 2, HEAD_ROWS, tokens), BF16),
        ],
        input_output_aliases={1: 0},
        compiler_params=params(),
        cost_estimate=cost(n),
    )(qe, acc, *kvs)


def last_kernel(qe_ref, acc_ref, *refs, n_refs, n_all, n):
    kv_refs, all_refs = refs[:n_refs], refs[n_refs : n_refs + n_all]
    out_ref, keys_ref, values_ref, sum_ref, both_ref, buf_ref, sem = refs[n_refs + n_all :]
    h = pl.program_id(1)

    @pl.when((pl.program_id(0) == 0) & (h == 0))
    def _():
        prepare(kv_refs, keys_ref, values_ref)

    query = qe_ref[0]
    sum_ref[...] = acc_ref[0]

    def step(slot, carry):
        sum_ref[...] += weigh(keys_ref[slot, h], values_ref[slot, h], query)
        return carry

    lax.fori_loop(0, n, step, 0)
    safe = jnp.max(jnp.where(sum_ref[HEAD_DIM : HEAD_DIM + 1, :] < LIMIT, 0.0, 1.0)) == 0.0

    @pl.when(jnp.logical_not(safe))
    def _():
        lane = lax.broadcasted_iota(jnp.int32, query.shape, 1)
        plain = jnp.where((lane // HEAD_DIM) == h, query, jnp.zeros_like(query))
        rows = buf_ref.shape[1]
        pieces = [(ref, g) for ref in all_refs for g in range(ref.shape[0])]
        sum_ref[...] = jnp.zeros_like(sum_ref)

        def piece(at, top):
            for index, (ref, g) in enumerate(pieces):

                @pl.when(at == index)
                def _(ref=ref, g=g):
                    copy = pltpu.make_async_copy(ref.at[g], buf_ref, sem)
                    copy.start()
                    copy.wait()

            scores = lax.dot_general(buf_ref[0], plain, NT, preferred_element_type=F32)
            higher = jnp.maximum(top, jnp.max(scores, axis=0, keepdims=True))
            probs = jnp.exp(scores - higher).astype(BF16)
            values = buf_ref[1].T
            values = jnp.where(h == 0, values[:HEAD_DIM], values[HEAD_DIM:])
            ones = jnp.ones((HEAD_ROWS - HEAD_DIM, rows), BF16)
            values = jnp.concatenate([values, ones], axis=0)
            part = jnp.dot(values, probs, preferred_element_type=F32)
            sum_ref[...] = sum_ref[...] * jnp.exp(top - higher) + part
            return higher

        lax.fori_loop(0, len(pieces), piece, jnp.full((1, query.shape[0]), -1e30, F32))

    both_ref[h] = sum_ref[:HEAD_DIM, :] / sum_ref[HEAD_DIM : HEAD_DIM + 1, :]

    @pl.when(h == 1)
    def _():
        joined = jnp.concatenate([both_ref[0], both_ref[1]], axis=0)
        out_ref[...] = joined.T.astype(BF16)


def last(qe, acc, kvs, all_kvs):
    n_all = len(all_kvs)
    tokens = qe.shape[1]
    n = blocks_of(kvs, tokens)
    tile = min(512, tokens)
    rows = kvs[0].shape[2]
    out = pl.pallas_call(
        functools.partial(last_kernel, n_refs=len(kvs), n_all=n_all, n=n),
        grid=(tokens // tile, 2),
        in_specs=[
            pl.BlockSpec((1, tile, LANES), lambda i, h: (h, i, 0)),
            pl.BlockSpec((1, HEAD_ROWS, tile), lambda i, h: (h, 0, i)),
        ]
        + [pl.BlockSpec(kv.shape, lambda i, h: (0, 0, 0, 0)) for kv in kvs]
        + [ANY] * n_all,
        out_specs=pl.BlockSpec((tile, LANES), lambda i, h: (i, 0)),
        out_shape=jax.ShapeDtypeStruct((tokens, LANES), BF16),
        scratch_shapes=[
            pltpu.VMEM((n, 2, tokens, LANES), BF16),
            pltpu.VMEM((n, 2, HEAD_ROWS, tokens), BF16),
            pltpu.VMEM((HEAD_ROWS, tile), F32),
            pltpu.VMEM((2, HEAD_DIM, tile), F32),
            pltpu.VMEM((2, rows, LANES), BF16),
            pltpu.SemaphoreType.DMA,
        ],
        compiler_params=params(),
        cost_estimate=cost(n),
    )(qe, acc, *kvs, *all_kvs)
    return out.reshape(tokens // rows, rows, LANES)


def swap(x, axis, bit):
    size = lax.axis_size(axis)
    return lax.ppermute(x, axis, [(i, i ^ bit) for i in range(size)])


def on_device(qkv):
    size = lax.axis_size("head")
    groups = size // 2
    rows = qkv.shape[0]
    width = qkv.shape[1] // 3
    pairs = width // groups // LANES
    bits = lax.axis_size("blk").bit_length() - 1
    rank = jnp.bitwise_and(lax.axis_index("head"), groups - 1).astype(jnp.int32).reshape(1)
    teams = [list(range(groups)), list(range(groups, size))]
    ranks = tuple(range(groups))

    def exchange(x):
        return lax.all_to_all(
            x, "head", split_axis=0, concat_axis=0, tiled=True, axis_index_groups=teams
        )

    order = [((1, 2), ranks), ((0,), ranks)] + [((1, 2), ((k,),)) for k in range(groups)]
    kv_all, q_all, *direct = pack(rank, qkv, 0, groups, order)
    far = [[swap(direct[k], "head", groups ^ k) for k in range(groups)]]
    own = [exchange(kv_all)]
    query = [exchange(q_all)[:, 0]]
    near = [[swap(own[0], "blk", 1 << bit) for bit in range(bits)]]
    for p in range(1, pairs):
        pieces = pack(rank, qkv, p, groups, [((0, 1, 2), ((k,),)) for k in range(groups)])
        pieces = [pieces[0]] + [swap(pieces[k], "head", k) for k in range(1, groups)]
        q, kv = merge(rank, pieces)
        query.append(q)
        own.append(kv)
        far.append([swap(kv, "head", groups)])
        near.append([swap(kv, "blk", 1 << bit) for bit in range(bits)])

    states = [first(query[p], own[p]) for p in range(pairs)]
    outs = []
    for p in range(pairs):
        qe, acc = states[p]
        everything = [own[p]] + near[p] + far[p]
        if p < pairs - 1:
            outs.append(last(qe, acc, near[p] + far[p], everything))
        else:
            acc = more(qe, acc, near[p])
            outs.append(last(qe, acc, far[p], everything))
    early = regroup(rank, outs[:-1])
    early = [early[0]] + [swap(early[k], "head", k) for k in range(1, groups)]
    result = place_early(rank, early, (rows, width))
    return place_last(rank, exchange(outs[-1]), result, pairs - 1)


def solution(mesh):
    spec = P(("blk", "head"), None)
    return jax.shard_map(on_device, mesh=mesh, in_specs=(spec,), out_specs=spec, check_vma=False)
```

```python
import functools

import jax
import jax.numpy as jnp
from jax import lax
from jax.experimental import pallas as pl
from jax.experimental.pallas import tpu as pltpu
from jax.sharding import PartitionSpec as P

HEAD_DIM = 64
LANES = 128
BLOCK = 2048
HEAD_ROWS = 80
LIMIT = 1e30
UNIT = 2e9
F32 = jnp.float32
BF16 = jnp.bfloat16
NT = (((1,), (1,)), ((), ()))
ANY = pl.BlockSpec(memory_space=pl.ANY)


def params(mib=58):
    return pltpu.CompilerParams(vmem_limit_bytes=mib << 20)


def cost(units):
    return pl.CostEstimate(flops=int(units * UNIT), bytes_accessed=1 << 20, transcendentals=0)


def staged(moves, buf_ref, in_sem, out_sem):
    reads = [pltpu.make_async_copy(s, buf_ref.at[n], in_sem) for n, (s, _) in enumerate(moves)]
    writes = [pltpu.make_async_copy(buf_ref.at[n], d, out_sem) for n, (_, d) in enumerate(moves)]
    for copy in reads:
        copy.start()
    for copy in reads:
        copy.wait()
    for copy in writes:
        copy.start()
    for copy in writes:
        copy.wait()


def move(kernel, rank, arrays, out_shape, n, rows, units, aliases=None):
    many = isinstance(out_shape, list)
    n_in, n_out = len(arrays), len(out_shape) if many else 1

    def body(rank_ref, *refs):
        ins, outs, rest = refs[:n_in], refs[n_in : n_in + n_out], refs[n_in + n_out :]
        staged(kernel(rank_ref[0], ins, outs), *rest)

    return pl.pallas_call(
        body,
        in_specs=[pl.BlockSpec(memory_space=pltpu.SMEM)] + [ANY] * n_in,
        out_specs=[ANY] * n_out if many else ANY,
        out_shape=out_shape,
        scratch_shapes=[
            pltpu.VMEM((n, rows, LANES), BF16),
            pltpu.SemaphoreType.DMA,
            pltpu.SemaphoreType.DMA,
        ],
        input_output_aliases=aliases or {},
        compiler_params=params(),
        cost_estimate=cost(units),
    )(rank, *arrays)


def pack(rank, qkv, first, groups, order):
    rows = qkv.shape[0]
    width = qkv.shape[1] // 3

    def kernel(me, ins, outs):
        moves = []
        for out, (kinds, dest) in zip(outs, order):
            for at, k in enumerate(dest):
                owner = k if isinstance(k, int) else jnp.bitwise_xor(me, k[0])
                start = pl.multiple_of(owner * (width // groups) + first * LANES, LANES)
                for n, kind in enumerate(kinds):
                    moves.append((ins[0].at[:, pl.ds(kind * width + start, LANES)], out.at[at, n]))
        return moves

    shapes = [(len(dest), len(kinds), rows, LANES) for kinds, dest in order]
    n = sum(shape[0] * shape[1] for shape in shapes)
    shapes = [jax.ShapeDtypeStruct(shape, BF16) for shape in shapes]
    return move(kernel, rank, [qkv], shapes, n, rows, 0.2)


def pack_last(rank, qkv, far, first):
    groups, _, rows, _ = far.shape
    width = qkv.shape[1] // 3

    def kernel(me, ins, outs):
        moves = []
        for k, out in enumerate(outs):
            owner = jnp.bitwise_xor(me, k)
            start = pl.multiple_of(owner * (width // groups) + first * LANES, LANES)
            for n in range(3):
                moves.append((ins[0].at[:, pl.ds(n * width + start, LANES)], out.at[0, n]))
            for n in range(2):
                moves.append((ins[1].at[owner, n], out.at[0, 3 + n]))
        return moves

    shapes = [jax.ShapeDtypeStruct((1, 5, rows, LANES), BF16)] * groups
    return move(kernel, rank, [qkv, far], shapes, 5 * groups, rows, 0.2)


def place(rank, pieces, pairs, base, shape):
    rows, _ = pieces[0][0].shape
    groups = len(pieces[0])
    width = shape[1] // groups
    flat = [piece for pair in pieces for piece in pair]
    n = len(flat)

    def kernel(me, ins, outs):
        moves = []
        for m, piece in enumerate(ins[:n]):
            owner = jnp.bitwise_xor(me, m % groups)
            start = pl.multiple_of(owner * width + pairs[m // groups] * LANES, LANES)
            moves.append((piece, outs[0].at[:, pl.ds(start, LANES)]))
        return moves

    out = jax.ShapeDtypeStruct(shape, BF16)
    if base is None:
        return move(kernel, rank, flat, out, n, rows, 0.2)
    return move(kernel, rank, flat + [base], out, n, rows, 0.2, {n + 1: 0})


def prepare(kv_refs, keys_ref, values_ref):
    tokens = keys_ref.shape[2]
    rows = kv_refs[0].shape[2]
    pieces = [(ref, g) for ref in kv_refs for g in range(ref.shape[0])]
    for n, (kv_ref, g) in enumerate(pieces):
        slot, at = divmod(n * rows, tokens)
        keys = kv_ref[g, 0]
        lane = lax.broadcasted_iota(jnp.int32, keys.shape, 1)
        one = jnp.ones_like(keys)
        span = pl.ds(at, rows)
        keys_ref[slot, 0, span, :] = jnp.where(lane < HEAD_DIM, keys, one)
        keys_ref[slot, 1, span, :] = jnp.where(lane < HEAD_DIM, one, keys)
        values = kv_ref[g, 1].T
        for h in range(2):
            values_ref[slot, h, :HEAD_DIM, span] = values[h * HEAD_DIM : (h + 1) * HEAD_DIM]
            values_ref[slot, h, HEAD_DIM:, span] = jnp.ones((HEAD_ROWS - HEAD_DIM, rows), BF16)


def weigh(keys, values, query):
    scores = lax.dot_general(keys, query, NT, preferred_element_type=F32)
    probs = jnp.exp(scores).astype(BF16)
    return jnp.dot(values, probs, preferred_element_type=F32)


def first_kernel(rank_ref, *refs, n, kinds):
    pieces, outs = refs[:n], refs[n:]
    joined, (qe_ref, acc_ref, query_ref, keys_ref, values_ref) = outs[: kinds // 2], outs[kinds // 2 :]
    i, h = pl.program_id(0), pl.program_id(1)

    @pl.when((i == 0) & (h == 0))
    def _():
        for k, piece in enumerate(pieces):
            query_ref[jnp.bitwise_xor(rank_ref[0], k)] = piece[0, 0]
            for m, out in enumerate(joined):
                out[k] = piece[0, 1 + 2 * m : 3 + 2 * m]
        prepare(joined[:1], keys_ref, values_ref)

    query = query_ref[i] * jnp.asarray(HEAD_DIM**-0.5, BF16)
    lane = lax.broadcasted_iota(jnp.int32, query.shape, 1)
    mine = (lane // HEAD_DIM) == h
    query = jnp.where(mine, query, jnp.zeros_like(query))
    probe = 256
    some = lax.dot_general(query, keys_ref[0, h, :probe, :], NT, preferred_element_type=F32)
    shift = -jnp.max(some, axis=1, keepdims=True)
    query = jnp.where(lane == (1 - h) * HEAD_DIM, shift.astype(BF16), query)
    qe_ref[0] = query
    acc_ref[0] = weigh(keys_ref[0, h], values_ref[0, h], query)


def first(rank, pieces):
    _, kinds, rows, _ = pieces[0].shape
    n = len(pieces)
    tokens = n * rows
    whole = (n, 2, rows, LANES)
    many = kinds // 2
    qe, acc = (2, tokens, LANES), (2, HEAD_ROWS, tokens)
    *kvs, qe, acc = pl.pallas_call(
        functools.partial(first_kernel, n=n, kinds=kinds),
        grid=(n, 2),
        in_specs=[pl.BlockSpec(memory_space=pltpu.SMEM)]
        + [pl.BlockSpec(pieces[0].shape, lambda i, h: (0, 0, 0, 0))] * n,
        out_specs=[pl.BlockSpec(whole, lambda i, h: (0, 0, 0, 0))] * many
        + [
            pl.BlockSpec((1, rows, LANES), lambda i, h: (h, i, 0)),
            pl.BlockSpec((1, HEAD_ROWS, rows), lambda i, h: (h, 0, i)),
        ],
        out_shape=[jax.ShapeDtypeStruct(whole, BF16)] * many
        + [jax.ShapeDtypeStruct(qe, BF16), jax.ShapeDtypeStruct(acc, F32)],
        scratch_shapes=[
            pltpu.VMEM((n, rows, LANES), BF16),
            pltpu.VMEM((1, 2, tokens, LANES), BF16),
            pltpu.VMEM((1, 2, HEAD_ROWS, tokens), BF16),
        ],
        compiler_params=params(),
        cost_estimate=cost(1),
    )(rank, *pieces)
    return kvs, (qe, acc)


def blocks_of(kvs, tokens):
    return sum(kv.shape[0] * kv.shape[2] for kv in kvs) // tokens


def more_kernel(qe_ref, acc_ref, *refs, n_refs, n):
    kv_refs, (out_ref, keys_ref, values_ref) = refs[:n_refs], refs[n_refs:]
    h = pl.program_id(1)

    @pl.when((pl.program_id(0) == 0) & (h == 0))
    def _():
        prepare(kv_refs, keys_ref, values_ref)

    query = qe_ref[0]
    out_ref[0] = acc_ref[0]

    def step(slot, carry):
        out_ref[0] += weigh(keys_ref[slot, h], values_ref[slot, h], query)
        return carry

    lax.fori_loop(0, n, step, 0)


def more(qe, acc, kvs):
    tokens = qe.shape[1]
    n = blocks_of(kvs, tokens)
    tile = kvs[0].shape[2]
    state = pl.BlockSpec((1, HEAD_ROWS, tile), lambda i, h: (h, 0, i))
    return pl.pallas_call(
        functools.partial(more_kernel, n_refs=len(kvs), n=n),
        grid=(tokens // tile, 2),
        in_specs=[pl.BlockSpec((1, tile, LANES), lambda i, h: (h, i, 0)), state]
        + [pl.BlockSpec(kv.shape, lambda i, h: (0, 0, 0, 0)) for kv in kvs],
        out_specs=state,
        out_shape=jax.ShapeDtypeStruct(acc.shape, F32),
        scratch_shapes=[
            pltpu.VMEM((n, 2, tokens, LANES), BF16),
            pltpu.VMEM((n, 2, HEAD_ROWS, tokens), BF16),
        ],
        input_output_aliases={1: 0},
        compiler_params=params(),
        cost_estimate=cost(n),
    )(qe, acc, *kvs)


def last_kernel(rank_ref, qe_ref, acc_ref, *refs, n_refs, n_all, n):
    kv_refs, all_refs = refs[:n_refs], refs[n_refs : n_refs + n_all]
    *out_refs, keys_ref, values_ref, sum_ref, both_ref, buf_ref, sem = refs[n_refs + n_all :]
    h = pl.program_id(1)

    @pl.when((pl.program_id(0) == 0) & (h == 0))
    def _():
        prepare(kv_refs, keys_ref, values_ref)

    query = qe_ref[0]
    sum_ref[...] = acc_ref[0]

    def step(slot, carry):
        sum_ref[...] += weigh(keys_ref[slot, h], values_ref[slot, h], query)
        return carry

    lax.fori_loop(0, n, step, 0)
    safe = jnp.max(jnp.where(sum_ref[HEAD_DIM : HEAD_DIM + 1, :] < LIMIT, 0.0, 1.0)) == 0.0

    @pl.when(jnp.logical_not(safe))
    def _():
        lane = lax.broadcasted_iota(jnp.int32, query.shape, 1)
        plain = jnp.where((lane // HEAD_DIM) == h, query, jnp.zeros_like(query))
        rows = buf_ref.shape[1]
        pieces = [(ref, g) for ref in all_refs for g in range(ref.shape[0])]
        sum_ref[...] = jnp.zeros_like(sum_ref)

        def piece(at, top):
            for index, (ref, g) in enumerate(pieces):

                @pl.when(at == index)
                def _(ref=ref, g=g):
                    copy = pltpu.make_async_copy(ref.at[g], buf_ref, sem)
                    copy.start()
                    copy.wait()

            scores = lax.dot_general(buf_ref[0], plain, NT, preferred_element_type=F32)
            higher = jnp.maximum(top, jnp.max(scores, axis=0, keepdims=True))
            probs = jnp.exp(scores - higher).astype(BF16)
            values = buf_ref[1].T
            values = jnp.where(h == 0, values[:HEAD_DIM], values[HEAD_DIM:])
            ones = jnp.ones((HEAD_ROWS - HEAD_DIM, rows), BF16)
            values = jnp.concatenate([values, ones], axis=0)
            part = jnp.dot(values, probs, preferred_element_type=F32)
            sum_ref[...] = sum_ref[...] * jnp.exp(top - higher) + part
            return higher

        lax.fori_loop(0, len(pieces), piece, jnp.full((1, query.shape[0]), -1e30, F32))

    both_ref[h] = sum_ref[:HEAD_DIM, :] / sum_ref[HEAD_DIM : HEAD_DIM + 1, :]

    @pl.when(h == 1)
    def _():
        joined = jnp.concatenate([both_ref[0], both_ref[1]], axis=0)
        joined = joined.T.astype(BF16)
        for k, out_ref in enumerate(out_refs):

            @pl.when(pl.program_id(0) == jnp.bitwise_xor(rank_ref[0], k))
            def _(out_ref=out_ref):
                out_ref[...] = joined


def last(rank, qe, acc, kvs, all_kvs):
    n_all = len(all_kvs)
    tokens = qe.shape[1]
    n = blocks_of(kvs, tokens)
    rows = kvs[0].shape[2]
    groups = tokens // rows
    return pl.pallas_call(
        functools.partial(last_kernel, n_refs=len(kvs), n_all=n_all, n=n),
        grid=(groups, 2),
        in_specs=[
            pl.BlockSpec(memory_space=pltpu.SMEM),
            pl.BlockSpec((1, rows, LANES), lambda i, h: (h, i, 0)),
            pl.BlockSpec((1, HEAD_ROWS, rows), lambda i, h: (h, 0, i)),
        ]
        + [pl.BlockSpec(kv.shape, lambda i, h: (0, 0, 0, 0)) for kv in kvs]
        + [ANY] * n_all,
        out_specs=[pl.BlockSpec((rows, LANES), lambda i, h: (0, 0))] * groups,
        out_shape=[jax.ShapeDtypeStruct((rows, LANES), BF16)] * groups,
        scratch_shapes=[
            pltpu.VMEM((n, 2, tokens, LANES), BF16),
            pltpu.VMEM((n, 2, HEAD_ROWS, tokens), BF16),
            pltpu.VMEM((HEAD_ROWS, rows), F32),
            pltpu.VMEM((2, HEAD_DIM, rows), F32),
            pltpu.VMEM((2, rows, LANES), BF16),
            pltpu.SemaphoreType.DMA,
        ],
        compiler_params=params(),
        cost_estimate=cost(n),
    )(rank, qe, acc, *kvs, *all_kvs)


def swap(x, axis, bit):
    size = lax.axis_size(axis)
    return lax.ppermute(x, axis, [(i, i ^ bit) for i in range(size)])


class Chain:
    def __init__(self):
        self.token = None

    def __call__(self, step, arrays, *rest):
        leaves, tree = jax.tree.flatten(arrays)
        if self.token is not None:
            self.token, *leaves = lax.optimization_barrier((self.token, *leaves))
        out = step(*jax.tree.unflatten(tree, leaves), *rest)
        self.token = jax.tree.leaves(out)[0]
        return out


def on_device(qkv):
    size = lax.axis_size("head")
    groups = size // 2
    rows = qkv.shape[0]
    width = qkv.shape[1] // 3
    pairs = width // groups // LANES
    bits = lax.axis_size("blk").bit_length() - 1
    rank = jnp.bitwise_and(lax.axis_index("head"), groups - 1).astype(jnp.int32).reshape(1)
    ranks = tuple(range(groups))
    chain = Chain()

    def spread(pieces, after=None):
        if after is not None:
            _, pieces = lax.optimization_barrier((after, pieces))
        return [pieces[0]] + [swap(pieces[k], "head", k) for k in range(1, groups)]

    def nearby(kv):
        return [swap(kv, "blk", 1 << bit) for bit in range(bits)]

    def fetch(p):
        if p < end:
            return chain(lambda r, x: pack(r, x, p, groups, each), (rank, qkv))
        return chain(lambda r, x, y: pack_last(r, x, y, end), (rank, qkv, raw))

    each = [((0, 1, 2), ((k,),)) for k in ranks]
    end = pairs - 1
    late = max(end - 1, 0)
    packed, pieces, own, near, far, state, returned = {}, {}, {}, {}, {}, {}, {}

    def open_(p):
        kvs, state[p] = chain(first, (rank, pieces[p]))
        own[p] = kvs[0]
        near[p] = nearby(own[p])
        if p == end:
            far[p] = kvs[1:]

    def cross(p):
        kv = own[p]
        before = raw if p == 0 else far[p - 1]
        _, _, kv = lax.optimization_barrier((before, chain.token, kv))
        far[p] = [swap(kv, "head", groups)]

    def grow(p):
        qe, acc = state[p]
        state[p] = qe, chain(more, (qe, acc, near[p]))

    def close(p, new):
        qe, acc = state[p]
        returned[p] = spread(chain(last, (rank, qe, acc, new, [own[p]] + near[p] + far[p])))

    (raw,) = chain(lambda r, x: pack(r, x, end, groups, [((1, 2), ranks)]), (rank, qkv))
    packed[0] = fetch(0)
    pieces[0] = spread(packed[0])
    for p in range(1, end):
        packed[p] = fetch(p)
    if end > 1:
        pieces[1] = spread(packed[1], pieces[0])
    _, raw = lax.optimization_barrier((pieces[min(1, late)], raw))
    raw = swap(raw, "head", groups)
    for p in range(end):
        open_(p)
        if p + 2 < end:
            pieces[p + 2] = spread(packed[p + 2], (pieces[p + 1], chain.token))
        cross(p)
        if p == late:
            pieces[end] = spread(fetch(end))
        if p > 0:
            grow(p - 1)
    grow(late)
    open_(end)
    if late > 0:
        close(0, far[0])
    close(end, near[end] + far[end])
    for p in range(1, end):
        close(p, far[p])
    if late == 0:
        close(0, far[0])
    early = [p for p in range(pairs) if p != late]
    shape = (rows, width)
    result = chain(lambda r, x: place(r, x, early, None, shape), (rank, [returned[p] for p in early]))
    return chain(lambda r, x, y: place(r, x, [late], y, shape), (rank, [returned[late]], result))


def solution(mesh):
    spec = P(("blk", "head"), None)
    return jax.shard_map(on_device, mesh=mesh, in_specs=(spec,), out_specs=spec, check_vma=False)
```

```python
import functools

import jax
import jax.numpy as jnp
from jax import lax
from jax.experimental import pallas as pl
from jax.experimental.pallas import tpu as pltpu
from jax.sharding import PartitionSpec as P

HEAD_DIM = 64
LANES = 128
BLOCK = 2048
HEAD_ROWS = 80
LIMIT = 1e30
UNIT = 2e9
F32 = jnp.float32
BF16 = jnp.bfloat16
NT = (((1,), (1,)), ((), ()))
ANY = pl.BlockSpec(memory_space=pl.ANY)


def params(mib=58):
    return pltpu.CompilerParams(vmem_limit_bytes=mib << 20)


def cost(units):
    return pl.CostEstimate(flops=int(units * UNIT), bytes_accessed=1 << 20, transcendentals=0)


def staged(moves, buf_ref, in_sem, out_sem):
    reads = [pltpu.make_async_copy(s, buf_ref.at[n], in_sem) for n, (s, _) in enumerate(moves)]
    writes = [pltpu.make_async_copy(buf_ref.at[n], d, out_sem) for n, (_, d) in enumerate(moves)]
    for copy in reads:
        copy.start()
    for copy in reads:
        copy.wait()
    for copy in writes:
        copy.start()
    for copy in writes:
        copy.wait()


def move(kernel, rank, arrays, out_shape, n, rows, units, aliases=None):
    many = isinstance(out_shape, list)
    n_in, n_out = len(arrays), len(out_shape) if many else 1

    def body(rank_ref, *refs):
        ins, outs, rest = refs[:n_in], refs[n_in : n_in + n_out], refs[n_in + n_out :]
        staged(kernel(rank_ref[0], ins, outs), *rest)

    return pl.pallas_call(
        body,
        in_specs=[pl.BlockSpec(memory_space=pltpu.SMEM)] + [ANY] * n_in,
        out_specs=[ANY] * n_out if many else ANY,
        out_shape=out_shape,
        scratch_shapes=[
            pltpu.VMEM((n, rows, LANES), BF16),
            pltpu.SemaphoreType.DMA,
            pltpu.SemaphoreType.DMA,
        ],
        input_output_aliases=aliases or {},
        compiler_params=params(),
        cost_estimate=cost(units),
    )(rank, *arrays)


def pack(rank, qkv, first, groups, order):
    rows = qkv.shape[0]
    width = qkv.shape[1] // 3

    def kernel(me, ins, outs):
        moves = []
        for out, (kinds, dest) in zip(outs, order):
            for at, k in enumerate(dest):
                owner = k if isinstance(k, int) else jnp.bitwise_xor(me, k[0])
                start = pl.multiple_of(owner * (width // groups) + first * LANES, LANES)
                for n, kind in enumerate(kinds):
                    moves.append((ins[0].at[:, pl.ds(kind * width + start, LANES)], out.at[at, n]))
        return moves

    shapes = [(len(dest), len(kinds), rows, LANES) for kinds, dest in order]
    n = sum(shape[0] * shape[1] for shape in shapes)
    shapes = [jax.ShapeDtypeStruct(shape, BF16) for shape in shapes]
    return move(kernel, rank, [qkv], shapes, n, rows, 0.2)


def pack_last(rank, qkv, far, first):
    groups, _, rows, _ = far.shape
    width = qkv.shape[1] // 3

    def kernel(me, ins, outs):
        moves = []
        for k, out in enumerate(outs):
            owner = jnp.bitwise_xor(me, k)
            start = pl.multiple_of(owner * (width // groups) + first * LANES, LANES)
            for n in range(3):
                moves.append((ins[0].at[:, pl.ds(n * width + start, LANES)], out.at[0, n]))
            for n in range(2):
                moves.append((ins[1].at[owner, n], out.at[0, 3 + n]))
        return moves

    shapes = [jax.ShapeDtypeStruct((1, 5, rows, LANES), BF16)] * groups
    return move(kernel, rank, [qkv, far], shapes, 5 * groups, rows, 0.2)


def place(rank, pieces, pairs, base, shape):
    rows, _ = pieces[0][0].shape
    groups = len(pieces[0])
    width = shape[1] // groups
    flat = [piece for pair in pieces for piece in pair]
    n = len(flat)

    def kernel(me, ins, outs):
        moves = []
        for m, piece in enumerate(ins[:n]):
            owner = jnp.bitwise_xor(me, m % groups)
            start = pl.multiple_of(owner * width + pairs[m // groups] * LANES, LANES)
            moves.append((piece, outs[0].at[:, pl.ds(start, LANES)]))
        return moves

    out = jax.ShapeDtypeStruct(shape, BF16)
    if base is None:
        return move(kernel, rank, flat, out, n, rows, 0.2)
    return move(kernel, rank, flat + [base], out, n, rows, 0.2, {n + 1: 0})


def prepare(kv_refs, keys_ref, values_ref):
    tokens = keys_ref.shape[2]
    rows = kv_refs[0].shape[2]
    pieces = [(ref, g) for ref in kv_refs for g in range(ref.shape[0])]
    for n, (kv_ref, g) in enumerate(pieces):
        slot, at = divmod(n * rows, tokens)
        keys = kv_ref[g, 0]
        lane = lax.broadcasted_iota(jnp.int32, keys.shape, 1)
        one = jnp.ones_like(keys)
        span = pl.ds(at, rows)
        keys_ref[slot, 0, span, :] = jnp.where(lane < HEAD_DIM, keys, one)
        keys_ref[slot, 1, span, :] = jnp.where(lane < HEAD_DIM, one, keys)
        values = kv_ref[g, 1].T
        for h in range(2):
            values_ref[slot, h, :HEAD_DIM, span] = values[h * HEAD_DIM : (h + 1) * HEAD_DIM]
            values_ref[slot, h, HEAD_DIM:, span] = jnp.ones((HEAD_ROWS - HEAD_DIM, rows), BF16)


def weigh(keys, values, query):
    scores = lax.dot_general(keys, query, NT, preferred_element_type=F32)
    probs = jnp.exp(scores).astype(BF16)
    return jnp.dot(values, probs, preferred_element_type=F32)


def first_kernel(rank_ref, *refs, n, kinds):
    pieces, outs = refs[:n], refs[n:]
    joined, (qe_ref, acc_ref, query_ref, keys_ref, values_ref) = outs[: kinds // 2], outs[kinds // 2 :]
    i, h = pl.program_id(0), pl.program_id(1)

    @pl.when((i == 0) & (h == 0))
    def _():
        for k, piece in enumerate(pieces):
            query_ref[jnp.bitwise_xor(rank_ref[0], k)] = piece[0, 0]
            for m, out in enumerate(joined):
                out[k] = piece[0, 1 + 2 * m : 3 + 2 * m]
        prepare(joined[:1], keys_ref, values_ref)

    query = query_ref[i] * jnp.asarray(HEAD_DIM**-0.5, BF16)
    lane = lax.broadcasted_iota(jnp.int32, query.shape, 1)
    mine = (lane // HEAD_DIM) == h
    query = jnp.where(mine, query, jnp.zeros_like(query))
    probe = 256
    some = lax.dot_general(query, keys_ref[0, h, :probe, :], NT, preferred_element_type=F32)
    shift = -jnp.max(some, axis=1, keepdims=True)
    query = jnp.where(lane == (1 - h) * HEAD_DIM, shift.astype(BF16), query)
    qe_ref[0] = query
    acc_ref[0] = weigh(keys_ref[0, h], values_ref[0, h], query)


def first(rank, pieces):
    _, kinds, rows, _ = pieces[0].shape
    n = len(pieces)
    tokens = n * rows
    whole = (n, 2, rows, LANES)
    many = kinds // 2
    qe, acc = (2, tokens, LANES), (2, HEAD_ROWS, tokens)
    *kvs, qe, acc = pl.pallas_call(
        functools.partial(first_kernel, n=n, kinds=kinds),
        grid=(n, 2),
        in_specs=[pl.BlockSpec(memory_space=pltpu.SMEM)]
        + [pl.BlockSpec(pieces[0].shape, lambda i, h: (0, 0, 0, 0))] * n,
        out_specs=[pl.BlockSpec(whole, lambda i, h: (0, 0, 0, 0))] * many
        + [
            pl.BlockSpec((1, rows, LANES), lambda i, h: (h, i, 0)),
            pl.BlockSpec((1, HEAD_ROWS, rows), lambda i, h: (h, 0, i)),
        ],
        out_shape=[jax.ShapeDtypeStruct(whole, BF16)] * many
        + [jax.ShapeDtypeStruct(qe, BF16), jax.ShapeDtypeStruct(acc, F32)],
        scratch_shapes=[
            pltpu.VMEM((n, rows, LANES), BF16),
            pltpu.VMEM((1, 2, tokens, LANES), BF16),
            pltpu.VMEM((1, 2, HEAD_ROWS, tokens), BF16),
        ],
        compiler_params=params(),
        cost_estimate=cost(1),
    )(rank, *pieces)
    return kvs, (qe, acc)


def blocks_of(kvs, tokens):
    return sum(kv.shape[0] * kv.shape[2] for kv in kvs) // tokens


def more_kernel(qe_ref, acc_ref, *refs, n_refs, n):
    kv_refs, (out_ref, keys_ref, values_ref) = refs[:n_refs], refs[n_refs:]

    @pl.when(pl.program_id(0) == 0)
    def _():
        prepare(kv_refs, keys_ref, values_ref)

    out_ref[...] = acc_ref[...]

    def step(slot, carry):
        for h in range(2):
            out_ref[h] += weigh(keys_ref[slot, h], values_ref[slot, h], qe_ref[h])
        return carry

    lax.fori_loop(0, n, step, 0)


def more(qe, acc, kvs):
    tokens = qe.shape[1]
    n = blocks_of(kvs, tokens)
    tile = kvs[0].shape[2]
    state = pl.BlockSpec((2, HEAD_ROWS, tile), lambda i: (0, 0, i))
    return pl.pallas_call(
        functools.partial(more_kernel, n_refs=len(kvs), n=n),
        grid=(tokens // tile,),
        in_specs=[pl.BlockSpec((2, tile, LANES), lambda i: (0, i, 0)), state]
        + [pl.BlockSpec(kv.shape, lambda i: (0, 0, 0, 0)) for kv in kvs],
        out_specs=state,
        out_shape=jax.ShapeDtypeStruct(acc.shape, F32),
        scratch_shapes=[
            pltpu.VMEM((n, 2, tokens, LANES), BF16),
            pltpu.VMEM((n, 2, HEAD_ROWS, tokens), BF16),
        ],
        input_output_aliases={1: 0},
        compiler_params=params(),
        cost_estimate=cost(n),
    )(qe, acc, *kvs)


def last_kernel(rank_ref, qe_ref, acc_ref, *refs, n_refs, n_all, n):
    kv_refs, all_refs = refs[:n_refs], refs[n_refs : n_refs + n_all]
    *out_refs, keys_ref, values_ref, sum_ref, both_ref, buf_ref, sem = refs[n_refs + n_all :]
    h = pl.program_id(1)

    @pl.when((pl.program_id(0) == 0) & (h == 0))
    def _():
        prepare(kv_refs, keys_ref, values_ref)

    query = qe_ref[0]
    sum_ref[...] = acc_ref[0]

    def step(slot, carry):
        sum_ref[...] += weigh(keys_ref[slot, h], values_ref[slot, h], query)
        return carry

    lax.fori_loop(0, n, step, 0)
    safe = jnp.max(jnp.where(sum_ref[HEAD_DIM : HEAD_DIM + 1, :] < LIMIT, 0.0, 1.0)) == 0.0

    @pl.when(jnp.logical_not(safe))
    def _():
        lane = lax.broadcasted_iota(jnp.int32, query.shape, 1)
        plain = jnp.where((lane // HEAD_DIM) == h, query, jnp.zeros_like(query))
        rows = buf_ref.shape[1]
        pieces = [(ref, g) for ref in all_refs for g in range(ref.shape[0])]
        sum_ref[...] = jnp.zeros_like(sum_ref)

        def piece(at, top):
            for index, (ref, g) in enumerate(pieces):

                @pl.when(at == index)
                def _(ref=ref, g=g):
                    copy = pltpu.make_async_copy(ref.at[g], buf_ref, sem)
                    copy.start()
                    copy.wait()

            scores = lax.dot_general(buf_ref[0], plain, NT, preferred_element_type=F32)
            higher = jnp.maximum(top, jnp.max(scores, axis=0, keepdims=True))
            probs = jnp.exp(scores - higher).astype(BF16)
            values = buf_ref[1].T
            values = jnp.where(h == 0, values[:HEAD_DIM], values[HEAD_DIM:])
            ones = jnp.ones((HEAD_ROWS - HEAD_DIM, rows), BF16)
            values = jnp.concatenate([values, ones], axis=0)
            part = jnp.dot(values, probs, preferred_element_type=F32)
            sum_ref[...] = sum_ref[...] * jnp.exp(top - higher) + part
            return higher

        lax.fori_loop(0, len(pieces), piece, jnp.full((1, query.shape[0]), -1e30, F32))

    both_ref[h] = sum_ref[:HEAD_DIM, :] / sum_ref[HEAD_DIM : HEAD_DIM + 1, :]

    @pl.when(h == 1)
    def _():
        joined = jnp.concatenate([both_ref[0], both_ref[1]], axis=0)
        joined = joined.T.astype(BF16)
        for k, out_ref in enumerate(out_refs):

            @pl.when(pl.program_id(0) == jnp.bitwise_xor(rank_ref[0], k))
            def _(out_ref=out_ref):
                out_ref[...] = joined


def last(rank, qe, acc, kvs, all_kvs):
    n_all = len(all_kvs)
    tokens = qe.shape[1]
    n = blocks_of(kvs, tokens)
    rows = kvs[0].shape[2]
    groups = tokens // rows
    return pl.pallas_call(
        functools.partial(last_kernel, n_refs=len(kvs), n_all=n_all, n=n),
        grid=(groups, 2),
        in_specs=[
            pl.BlockSpec(memory_space=pltpu.SMEM),
            pl.BlockSpec((1, rows, LANES), lambda i, h: (h, i, 0)),
            pl.BlockSpec((1, HEAD_ROWS, rows), lambda i, h: (h, 0, i)),
        ]
        + [pl.BlockSpec(kv.shape, lambda i, h: (0, 0, 0, 0)) for kv in kvs]
        + [ANY] * n_all,
        out_specs=[pl.BlockSpec((rows, LANES), lambda i, h: (0, 0))] * groups,
        out_shape=[jax.ShapeDtypeStruct((rows, LANES), BF16)] * groups,
        scratch_shapes=[
            pltpu.VMEM((n, 2, tokens, LANES), BF16),
            pltpu.VMEM((n, 2, HEAD_ROWS, tokens), BF16),
            pltpu.VMEM((HEAD_ROWS, rows), F32),
            pltpu.VMEM((2, HEAD_DIM, rows), F32),
            pltpu.VMEM((2, rows, LANES), BF16),
            pltpu.SemaphoreType.DMA,
        ],
        compiler_params=params(),
        cost_estimate=cost(n),
    )(rank, qe, acc, *kvs, *all_kvs)


def swap(x, axis, bit):
    size = lax.axis_size(axis)
    return lax.ppermute(x, axis, [(i, i ^ bit) for i in range(size)])


class Chain:
    def __init__(self):
        self.token = None

    def __call__(self, step, arrays, *rest):
        leaves, tree = jax.tree.flatten(arrays)
        if self.token is not None:
            self.token, *leaves = lax.optimization_barrier((self.token, *leaves))
        out = step(*jax.tree.unflatten(tree, leaves), *rest)
        self.token = jax.tree.leaves(out)[0]
        return out


def on_device(qkv):
    size = lax.axis_size("head")
    groups = size // 2
    rows = qkv.shape[0]
    width = qkv.shape[1] // 3
    pairs = width // groups // LANES
    bits = lax.axis_size("blk").bit_length() - 1
    rank = jnp.bitwise_and(lax.axis_index("head"), groups - 1).astype(jnp.int32).reshape(1)
    ranks = tuple(range(groups))
    chain = Chain()

    def spread(pieces, after=None):
        if after is not None:
            _, pieces = lax.optimization_barrier((after, pieces))
        return [pieces[0]] + [swap(pieces[k], "head", k) for k in range(1, groups)]

    def nearby(kv):
        return [swap(kv, "blk", 1 << bit) for bit in range(bits)]

    def fetch(p):
        if p < end:
            return chain(lambda r, x: pack(r, x, p, groups, each), (rank, qkv))
        return chain(lambda r, x, y: pack_last(r, x, y, end), (rank, qkv, raw))

    each = [((0, 1, 2), ((k,),)) for k in ranks]
    end = pairs - 1
    late = max(end - 1, 0)
    packed, pieces, own, near, far, state, returned = {}, {}, {}, {}, {}, {}, {}

    def open_(p):
        kvs, state[p] = chain(first, (rank, pieces[p]))
        own[p] = kvs[0]
        near[p] = nearby(own[p])
        if p == end:
            far[p] = kvs[1:]

    def cross(p):
        kv = own[p]
        before = raw if p == 0 else far[p - 1]
        _, _, kv = lax.optimization_barrier((before, chain.token, kv))
        far[p] = [swap(kv, "head", groups)]

    def grow(p):
        qe, acc = state[p]
        state[p] = qe, chain(more, (qe, acc, near[p]))

    def close(p, new):
        qe, acc = state[p]
        returned[p] = spread(chain(last, (rank, qe, acc, new, [own[p]] + near[p] + far[p])))

    (raw,) = chain(lambda r, x: pack(r, x, end, groups, [((1, 2), ranks)]), (rank, qkv))
    packed[0] = fetch(0)
    pieces[0] = spread(packed[0])
    for p in range(1, end):
        packed[p] = fetch(p)
    if end > 1:
        pieces[1] = spread(packed[1], pieces[0])
    _, raw = lax.optimization_barrier((pieces[min(1, late)], raw))
    raw = swap(raw, "head", groups)
    for p in range(end):
        open_(p)
        if p + 2 < end:
            pieces[p + 2] = spread(packed[p + 2], (pieces[p + 1], chain.token))
        cross(p)
        if p == late:
            pieces[end] = spread(fetch(end))
        if p > 0:
            grow(p - 1)
    grow(late)
    open_(end)
    if late > 0:
        close(0, far[0])
    close(end, near[end] + far[end])
    for p in range(1, end):
        close(p, far[p])
    if late == 0:
        close(0, far[0])
    early = [p for p in range(pairs) if p != late]
    shape = (rows, width)
    result = chain(lambda r, x: place(r, x, early, None, shape), (rank, [returned[p] for p in early]))
    return chain(lambda r, x, y: place(r, x, [late], y, shape), (rank, [returned[late]], result))


def solution(mesh):
    spec = P(("blk", "head"), None)
    return jax.shard_map(on_device, mesh=mesh, in_specs=(spec,), out_specs=spec, check_vma=False)
```
